128 devices in a mesh: row: 8 (over z, core), col: 16 (over y, x).
Axes of the slice: x: 4, y: 4, z: 4, core: 2. Of those that a mesh axis runs over, the one named last changes fastest.
Arguments:
- modes: bfloat16 [384, 65536], P('col', 'row'), may hold values from -6 to 6
- atom_site: int32 [65536, 1], P(('row', 'col')), may hold values from 0 to 15, as said below
- site_owner: int32 [16], replicated, may hold values from 0 to 7, as said below
- translation: int32 [65536], P(('row', 'col')), may hold values from 0 to 12166, as said below
- wavevectors: int32 [4096], P('col'), may hold values from 0 to 12166
Outputs:
- projected: float32 [16, 128, 4096], P('row', None, 'col')
- unfolded: float32 [128, 4096], P('row', 'col')
The draws below stay inside these ranges and needn't reach their ends.
Inputs may be any that keep to these rules, and one draw needn't show every extreme that they name: `atom_site`: among the atoms of one device (aligned blocks of 512 atoms) no site appears more than 64 times, and some site appears exactly 64 times. `site_owner`: every index of row owns exactly 2 sites. `translation`: the atoms of one site sit on distinct cells.
All inputs are finite; a program needn't handle non-finite values.
Results may differ from the reference program's by a relative error of at most 0.0028.
Values may be sent and summed in bfloat16 or wider, within the bound.
No kernel may reach another device: no remote copies, remote signals or barrier semaphores. Data moves between devices by JAX's collectives and lax.ppermute only.
A program may use at most 128 MiB of HBM per device.

```python
import math
import jax
import jax.numpy as jnp
from jax import lax

MODES = 128
KPTS = 4096
EDGE = 23
SITE_DEV = 2
ATOM_DEV = 512
SITES = 16
CAP = 64
ATOMS = 65536
N_ROW = 8
N_COL = 16


def draw_lattice(key):
    block_count = ATOMS // ATOM_DEV
    cell_count = EDGE * EDGE * EDGE
    key_bias, key_noise, key_order, key_cells = jax.random.split(key, 4)
    labels = jnp.arange(SITES, dtype=jnp.int32)
    bias = jax.random.permutation(key_bias, SITES).astype(jnp.int32)
    noise = jax.random.randint(key_noise, (block_count, SITES), 0, SITES, dtype=jnp.int32)
    score = (noise + bias[None, :]) * SITES + labels[None, :]
    unused, chosen = lax.top_k(score, SITES // 2)
    site_list = jnp.repeat(chosen.astype(jnp.int32), CAP, axis=1)
    order_keys = jax.random.randint(key_order, (block_count, ATOM_DEV), 0, 1 << 20, dtype=jnp.int32)
    order_keys = order_keys * ATOM_DEV + jnp.arange(ATOM_DEV, dtype=jnp.int32)[None, :]
    shuffle = jnp.argsort(order_keys, axis=1).astype(jnp.int32)
    site_ids = jnp.take_along_axis(site_list, shuffle, axis=1).reshape(-1)
    onehot = (site_ids[:, None] == labels[None, :]).astype(jnp.int32)
    ranking = jnp.sum((jnp.cumsum(onehot, axis=0) - onehot) * onehot, axis=1)
    cell_keys = jax.random.randint(key_cells, (SITES, cell_count), 0, 1 << 20, dtype=jnp.int32)
    cell_keys = cell_keys * cell_count + jnp.arange(cell_count, dtype=jnp.int32)[None, :]
    table = jnp.argsort(cell_keys, axis=1).astype(jnp.int32)
    cells = table[site_ids, ranking].astype(jnp.int32)
    return (site_ids.astype(jnp.int32), cells)


def draw_atom_site(key, part):
    site_ids, cells = draw_lattice(key)
    return site_ids[:, None]


def draw_translation(key, part):
    site_ids, cells = draw_lattice(key)
    return cells


def draw_site_owner(key, part):
    key = jax.random.fold_in(key, 5)
    shuffled = jax.random.permutation(key, SITES)
    return (shuffled // SITE_DEV).astype(jnp.int32)


def set_ends(result, rng, least, largest):
    spot = [jax.random.randint(jax.random.fold_in(rng, axis), (), 0, length) for axis, length in enumerate(result.shape)]
    main_axis = result.shape.index(max(result.shape))
    neighbour = spot[:main_axis] + [(spot[main_axis] + 1) % result.shape[main_axis]] + spot[main_axis + 1:]
    return result.at[tuple(spot)].set(least).at[tuple(neighbour)].set(largest)


def with_spikes(entries, key, source, target, blocks, factor):
    def block_of(dim):
        return (jnp.arange(entries.shape[dim]) // (entries.shape[dim] // blocks)).reshape((-1,) + (1,) * (entries.ndim - 1 - dim))

    near = jax.random.permutation(key, blocks)[block_of(target)]
    other_side = (block_of(target) + blocks // 2) % blocks
    return jnp.where((block_of(source) == near) | (block_of(source) == other_side), factor * entries, entries)


def block_scale(key, dims, shards, low, largest):
    gain, own = 1.0, jax.random.fold_in(key, 6)
    for position, shards_of in shards:
        steps = jnp.exp(jax.random.uniform(jax.random.fold_in(own, position), (shards_of,), jnp.float32, low / len(shards), largest / len(shards)))
        gain = gain * jnp.repeat(steps, dims[position] // shards_of).reshape([-1 if axis == position else 1 for axis in range(len(dims))])
    return gain


def bell_draw_with(key, extent, width, limit, cuts, heavy, kind=jnp.bfloat16):
    drawn = width * jax.random.normal(key, extent, jnp.float32)
    if cuts:
        drawn = drawn * block_scale(key, extent, cuts, -0.22, 0.18)
    return jnp.clip(with_spikes(drawn, jax.random.fold_in(key, 3), *heavy), -limit, limit).astype(kind)


def setup_inputs(seed: int = 0) -> dict:
    splits = jax.random.split(jax.random.key(seed), 6)
    modes = bell_draw_with(splits[0], (3 * MODES, ATOMS), 1.0, 6.0, ((0, 16), (1, 8)), (1, 0, 16, 2.0))
    atom_site = draw_atom_site(jax.random.fold_in(splits[5], 71), 0)
    site_owner = draw_site_owner(jax.random.fold_in(splits[5], 71), 0)
    translation = draw_translation(jax.random.fold_in(splits[5], 71), 0)
    wavevectors = set_ends(jax.random.randint(splits[4], (KPTS,), 0, EDGE * EDGE * EDGE), jax.random.fold_in(splits[4], 1), 0, (EDGE * EDGE * EDGE) - 1).astype(jnp.int32)
    return dict(modes=modes, atom_site=atom_site, site_owner=site_owner, translation=translation, wavevectors=wavevectors)


def phase_tile(cells, vectors):
    cell_a = cells // (EDGE * EDGE)
    cell_b = (cells // EDGE) % EDGE
    cell_c = cells % EDGE
    wave_a = vectors // (EDGE * EDGE)
    wave_b = (vectors // EDGE) % EDGE
    wave_c = vectors % EDGE
    turns = (cell_a[:, None] * wave_a[None, :] + cell_b[:, None] * wave_b[None, :] + cell_c[:, None] * wave_c[None, :]) % EDGE
    angle = turns.astype(jnp.float32) * (2.0 * math.pi / EDGE)
    return jnp.concatenate([jnp.cos(angle), jnp.sin(angle)], axis=1).astype(jnp.bfloat16)


def reference(modes, atom_site, site_owner, translation, wavevectors):
    device_count = N_ROW * N_COL
    site_ids = atom_site[:, 0]
    blocks = site_ids.reshape(device_count, ATOM_DEV)
    labels = jnp.arange(SITES, dtype=jnp.int32)
    onehot = (blocks[:, :, None] == labels[None, None, :]).astype(jnp.int32)
    before = jnp.sum((jnp.cumsum(onehot, axis=1) - onehot) * onehot, axis=2)
    device_ids = jnp.arange(device_count, dtype=jnp.int32)[:, None]
    flat_slots = (blocks * (device_count * CAP) + device_ids * CAP + before).reshape(-1)
    per_site = device_count * CAP
    slotted = jnp.zeros((3 * MODES, SITES * per_site), jnp.bfloat16).at[:, flat_slots].set(modes)
    stacked = slotted.reshape(3 * MODES, SITES, per_site).transpose(1, 0, 2)
    cell_slots = jnp.zeros((SITES * per_site,), jnp.int32).at[flat_slots].set(translation).reshape(SITES, per_site)
    norm_value = 3.0 * ATOM_DEV * N_COL / SITE_DEV

    def one_site(pair):
        columns, cells = pair
        tiles = phase_tile(cells, wavevectors)
        amplitude = jnp.dot(columns, tiles, preferred_element_type=jnp.float32)
        power = amplitude[:, :KPTS] ** 2 + amplitude[:, KPTS:] ** 2
        return jnp.sum(power.reshape(3, MODES, KPTS), axis=0) / norm_value

    results = lax.map(one_site, (stacked, cell_slots))
    same_owner = site_owner[:, None] == site_owner[None, :]
    earlier = labels[:, None] > labels[None, :]
    within = jnp.sum((same_owner & earlier).astype(jnp.int32), axis=1)
    order_index = site_owner * SITE_DEV + within
    projected = jnp.zeros_like(results).at[order_index].set(results)
    unfolded = jnp.sum(projected, axis=0) / SITES
    return projected, unfolded
```

```python
import functools
import math

import jax
import jax.numpy as jnp
import numpy as np
from jax import lax
from jax.experimental import pallas as pl
from jax.experimental.pallas import tpu as pltpu
from jax.sharding import PartitionSpec as P

EDGE = 23
HALF = 12
F32, BF16, I32 = jnp.float32, jnp.bfloat16, jnp.int32
CELL_BITS = 14
PANEL = 32
GROUP = 2048
ROWS_LHS = 560
LANES = 384
NT = (((1,), (1,)), ((), ()))


def split_flat(flat):
    first = jnp.floor((flat + 0.5) * (1.0 / (EDGE * EDGE)))
    rest = flat - first * (EDGE * EDGE)
    second = jnp.floor((rest + 0.5) * (1.0 / EDGE))
    return first, second, rest - second * EDGE


def trig_table():
    coord = np.arange(32)
    wave = np.arange(24)
    angle = 2.0 * math.pi * ((wave[:, None] * coord[None, :]) % EDGE) / EDGE
    cos, sin = np.cos(angle), np.sin(angle)
    axes = [
        (0, np.concatenate([cos[:HALF], sin[1:HALF], np.zeros((1, 32))])),
        (24, np.concatenate([cos, sin])),
        (72, np.concatenate([cos[:HALF], sin[:HALF]])),
    ]
    table = np.zeros((96, 192), np.float64)
    for axis, (start, part) in enumerate(axes):
        high = part.astype(jnp.bfloat16).astype(np.float64)
        table[start : start + len(part), axis * 64 : axis * 64 + 32] = high
        table[start : start + len(part), axis * 64 + 32 : axis * 64 + 64] = part - high
    return table.astype(jnp.bfloat16)


def bucket_kernel(owner_ref, modes_ref, meta_ref, out_ref, acc_ref):
    sites = owner_ref.shape[0]
    blocks, block = meta_ref.shape
    owners = sites // 2
    order = []
    for s in range(sites):
        within = jnp.int32(0)
        for earlier in range(s):
            within += (owner_ref[earlier] == owner_ref[s]).astype(I32)
        order.append(owner_ref[s] * 2 + within)
    meta = meta_ref[...]
    site = lax.shift_right_logical(meta, CELL_BITS)
    coords = split_flat((meta & (2**CELL_BITS - 1)).astype(F32))
    hot = [(site == s).astype(F32) for s in range(sites)]
    stacked = jnp.concatenate(hot, axis=0).astype(BF16)
    source = lax.broadcasted_iota(I32, (block, block), 0)
    target = lax.broadcasted_iota(I32, (block, block), 1)
    earlier = (source < target).astype(F32).astype(BF16)
    before = jnp.dot(stacked, earlier, preferred_element_type=F32)
    per_group = GROUP // block
    upper = lax.broadcasted_iota(I32, (sites * blocks, sites * blocks), 0)
    lower = lax.broadcasted_iota(I32, (sites * blocks, sites * blocks), 1)
    same = (upper // per_group == lower // per_group) & (lower < upper)
    offsets = jnp.sum(
        jnp.dot(same.astype(F32).astype(BF16), stacked, preferred_element_type=F32), axis=1, keepdims=True
    )
    before = before + offsets
    rank = jnp.zeros(meta.shape, F32)
    place = jnp.zeros(meta.shape, F32)
    for s in range(sites):
        rank += hot[s] * before[s * blocks : (s + 1) * blocks]
        place += hot[s] * order[s].astype(F32)
    slots = GROUP // 8
    slot_iota = lax.broadcasted_iota(I32, (slots, block), 0).astype(F32)
    pad = jnp.zeros((5, block), F32)
    for group in range(blocks // per_group):
        total = None
        for part in range(per_group):
            b = group * per_group + part
            rows = [c[b : b + 1] for c in coords]
            panel = jnp.concatenate([modes_ref[:, b * block : (b + 1) * block].astype(F32), *rows, pad], axis=0)
            place_row = place[b : b + 1]
            left = jnp.concatenate(
                [jnp.where(place_row == p, panel, 0.0).astype(BF16) for p in range(sites)], axis=0
            )
            right = (slot_iota == rank[b : b + 1]).astype(F32).astype(BF16)
            product = lax.dot_general(left, right, NT, preferred_element_type=F32)
            total = product if total is None else total + product
        for p in range(sites):
            piece = total[p * PANEL : (p + 1) * PANEL].astype(BF16)
            out_ref[p % 2, p // 2, :, group * slots : (group + 1) * slots] = piece


def bucket(owner, modes, meta):
    blocks, block = meta.shape
    owners = owner.shape[0] // 2
    slots = blocks * block // 8
    return pl.pallas_call(
        bucket_kernel,
        out_shape=jax.ShapeDtypeStruct((2, owners, PANEL, slots), BF16),
        in_specs=[
            pl.BlockSpec(memory_space=pltpu.SMEM),
            pl.BlockSpec(memory_space=pltpu.VMEM),
            pl.BlockSpec(memory_space=pltpu.VMEM),
        ],
        out_specs=pl.BlockSpec(memory_space=pltpu.VMEM),
        scratch_shapes=[pltpu.VMEM((8, 128), F32)],
        compiler_params=pltpu.CompilerParams(vmem_limit_bytes=48 * 2**20),
        cost_estimate=pl.CostEstimate(flops=4 * 10**9, bytes_accessed=1500000, transcendentals=0),
    )(owner, modes, meta)


def fill(panel_ref, chunk, table, trig_ref, left_ref, right_ref):
    panel = panel_ref[chunk].astype(F32)
    width = panel.shape[1]
    coord = lax.broadcasted_iota(I32, (32, width), 0).astype(F32)
    hot = []
    for axis in range(3):
        one = (coord == panel[24 + axis : 25 + axis]).astype(F32).astype(BF16)
        hot += [one, one]
    trig_ref[...] = jnp.dot(table, jnp.concatenate(hot, axis=0), preferred_element_type=F32)
    values = panel[:24]
    for pair in range(HALF):
        first = values * trig_ref[2 * pair : 2 * pair + 1]
        if pair < HALF - 1:
            second = values * trig_ref[2 * pair + 1 : 2 * pair + 2]
        else:
            second = jnp.zeros((8, width), F32)
        both = jnp.concatenate([first, second], axis=0).astype(BF16)
        left_ref[48 * pair : 48 * pair + both.shape[0]] = both
    cos1, sin1 = trig_ref[24:48], trig_ref[48:72]
    for pair in range(HALF // 2):
        cos_parts, sin_parts = [], []
        for wave in (2 * pair, 2 * pair + 1):
            cos2, sin2 = trig_ref[72 + wave : 73 + wave], trig_ref[84 + wave : 85 + wave]
            cos_parts.append(cos1 * cos2 - sin1 * sin2)
            sin_parts.append(sin1 * cos2 + cos1 * sin2)
        right_ref[48 * pair : 48 * pair + 48] = jnp.concatenate(cos_parts, axis=0).astype(BF16)
        right_ref[LANES + 48 * pair : LANES + 48 * pair + 48] = jnp.concatenate(sin_parts, axis=0).astype(BF16)


def project_kernel(norm, panel_ref, wave_ref, table_ref, out_ref, trig_ref, left0, left1, right0, right1, acc_ref, power_ref):
    lefts, rights = (left0, left1), (right0, right1)
    chunks = panel_ref.shape[0]
    table = table_ref[...]
    for right in rights:
        right[288:LANES] = jnp.zeros((LANES - 288, right.shape[1]), BF16)
        right[LANES + 288 :] = jnp.zeros((LANES - 288, right.shape[1]), BF16)
    for chunk in range(chunks):
        fill(panel_ref, chunk, table, trig_ref, lefts[chunk % 2], rights[chunk % 2])
        product = lax.dot_general(lefts[chunk % 2][...], rights[chunk % 2][...], NT, preferred_element_type=F32)
        if chunk == 0:
            acc_ref[...] = product
        else:
            acc_ref[...] += product
    scale = 1.0 / norm
    for wave in range(HALF):
        cc = acc_ref[24 * wave : 24 * wave + 24, :LANES]
        cs = acc_ref[24 * wave : 24 * wave + 24, LANES:]
        if wave:
            sc = acc_ref[24 * (11 + wave) : 24 * (12 + wave), :LANES]
            ss = acc_ref[24 * (11 + wave) : 24 * (12 + wave), LANES:]
            same = ((cc - ss) ** 2 + (cs + sc) ** 2) * scale
            other = ((cc + ss) ** 2 + (cs - sc) ** 2) * scale
        else:
            same = other = (cc**2 + cs**2) * scale
        power_ref[48 * wave : 48 * wave + 48] = jnp.concatenate([same, other], axis=0).astype(BF16)
    dests, width = wave_ref.shape
    first, second, third = split_flat(wave_ref[...].astype(F32))
    flip0 = first > HALF - 1
    flip2 = third > HALF - 1
    wave0 = jnp.where(flip0, EDGE - first, first)
    wave1 = jnp.where(flip2 & (second > 0), EDGE - second, second)
    wave2 = jnp.where(flip2, EDGE - third, third)
    column = wave2 * 24.0 + wave1
    group = wave0 * 2.0 + (flip0 != flip2).astype(F32)
    row_iota = lax.broadcasted_iota(I32, (LANES, width), 0).astype(F32)
    for dest in range(dests):
        pick = (row_iota == column[dest : dest + 1]).astype(F32).astype(BF16)
        picked = jnp.dot(power_ref[...], pick, preferred_element_type=F32)
        total = jnp.zeros((24, width), F32)
        for g in range(2 * HALF):
            total += jnp.where(group[dest : dest + 1] == g, picked[24 * g : 24 * g + 24], 0.0)
        out_ref[dest] = total.astype(BF16)


def project(panel, waves, norm):
    sources, rows, slots = panel.shape
    table = jnp.asarray(trig_table())
    return pl.pallas_call(
        functools.partial(project_kernel, norm),
        out_shape=jax.ShapeDtypeStruct((waves.shape[0], 24, waves.shape[1]), BF16),
        in_specs=[pl.BlockSpec(memory_space=pltpu.VMEM)] * 3,
        out_specs=pl.BlockSpec(memory_space=pltpu.VMEM),
        scratch_shapes=[
            pltpu.VMEM((96, slots), F32),
            pltpu.VMEM((ROWS_LHS, slots), BF16),
            pltpu.VMEM((ROWS_LHS, slots), BF16),
            pltpu.VMEM((2 * LANES, slots), BF16),
            pltpu.VMEM((2 * LANES, slots), BF16),
            pltpu.VMEM((ROWS_LHS, 2 * LANES), F32),
            pltpu.VMEM((576, LANES), BF16),
        ],
        compiler_params=pltpu.CompilerParams(vmem_limit_bytes=48 * 2**20),
        cost_estimate=pl.CostEstimate(flops=9 * 10**9, bytes_accessed=1000000, transcendentals=0),
    )(panel, waves, table)


def body(modes, atom_site, site_owner, translation, wavevectors):
    col_count = lax.axis_size("col")
    sites = site_owner.shape[0]
    atoms = translation.shape[0]
    norm = 3.0 * atoms * col_count / 2.0
    packed = jnp.concatenate([atom_site[:, 0] * 2**CELL_BITS + translation, wavevectors])
    packed = jnp.broadcast_to(packed[None], (col_count, packed.shape[0]))
    gathered = lax.all_to_all(packed, "col", split_axis=0, concat_axis=0, tiled=True)
    meta, waves = gathered[:, :atoms], gathered[:, atoms:]
    buckets = bucket(site_owner, modes, meta)
    pieces = []
    for place in range(2):
        panel = lax.all_to_all(buckets[place], "row", split_axis=0, concat_axis=0, tiled=True)
        power = project(panel, waves, norm)
        arrived = lax.all_to_all(power, "col", split_axis=0, concat_axis=0, tiled=True)
        pieces.append(jnp.sum(arrived.astype(F32).reshape(3, -1, arrived.shape[2]), axis=0))
    projected = jnp.stack(pieces)
    local = jnp.sum(projected, axis=0).reshape(lax.axis_size("row"), -1, wavevectors.shape[0])
    shares = lax.all_to_all(local, "row", split_axis=0, concat_axis=0, tiled=True)
    return projected, jnp.sum(shares, axis=0) / sites


def solution(mesh):
    placed = (P("col", "row"), P(("row", "col"), None), P(), P(("row", "col")), P("col"))
    return jax.shard_map(
        body,
        mesh=mesh,
        in_specs=placed,
        out_specs=(P("row", None, "col"), P("row", "col")),
        check_vma=False,
    )
```

```python
import functools
import math

import jax
import jax.numpy as jnp
import numpy as np
from jax import lax
from jax.experimental import pallas as pl
from jax.experimental.pallas import tpu as pltpu
from jax.sharding import PartitionSpec as P

EDGE = 23
HALF = 12
F32, BF16, I32 = jnp.float32, jnp.bfloat16, jnp.int32
CELL_BITS = 14
PANEL = 32
GROUP = 2048
ROWS_LHS = 560
LANES = 384
NT = (((1,), (1,)), ((), ()))


def split_flat(flat):
    first = jnp.floor((flat + 0.5) * (1.0 / (EDGE * EDGE)))
    rest = flat - first * (EDGE * EDGE)
    second = jnp.floor((rest + 0.5) * (1.0 / EDGE))
    return first, second, rest - second * EDGE


def sine_terms():
    nodes = 0.25 * np.cos(np.pi * (np.arange(400) + 0.5) / 800.0)
    turn = 2.0 * nodes
    return [float(c) for c in np.polyfit(turn**2, np.sin(2.0 * np.pi * turn) / turn, 6)]


SINE = sine_terms()


def sine(turn):
    square = turn * turn
    total = SINE[0]
    for term in SINE[1:]:
        total = total * square + term
    return total * turn


def bucket_kernel(owner_ref, modes_ref, meta_ref, out_ref):
    sites = owner_ref.shape[0]
    blocks, block = meta_ref.shape
    order = []
    for s in range(sites):
        within = jnp.int32(0)
        for earlier in range(s):
            within += (owner_ref[earlier] == owner_ref[s]).astype(I32)
        order.append(owner_ref[s] * 2 + within)
    meta = meta_ref[...]
    site = lax.shift_right_logical(meta, CELL_BITS)
    coords = split_flat((meta & (2**CELL_BITS - 1)).astype(F32))
    hot = [(site == s).astype(F32) for s in range(sites)]
    stacked = jnp.concatenate(hot, axis=0).astype(BF16)
    source = lax.broadcasted_iota(I32, (block, block), 0)
    target = lax.broadcasted_iota(I32, (block, block), 1)
    earlier = (source < target).astype(F32).astype(BF16)
    before = jnp.dot(stacked, earlier, preferred_element_type=F32)
    per_group = GROUP // block
    upper = lax.broadcasted_iota(I32, (sites * blocks, sites * blocks), 0)
    lower = lax.broadcasted_iota(I32, (sites * blocks, sites * blocks), 1)
    same = (upper // per_group == lower // per_group) & (lower < upper)
    offsets = jnp.sum(
        jnp.dot(same.astype(F32).astype(BF16), stacked, preferred_element_type=F32), axis=1, keepdims=True
    )
    before = before + offsets
    rank = jnp.zeros(meta.shape, F32)
    place = jnp.zeros(meta.shape, F32)
    for s in range(sites):
        rank += hot[s] * before[s * blocks : (s + 1) * blocks]
        place += hot[s] * order[s].astype(F32)
    slots = GROUP // 8
    slot_iota = lax.broadcasted_iota(I32, (slots, block), 0).astype(F32)
    pad = jnp.zeros((5, block), F32)
    for group in range(blocks // per_group):
        total = None
        for part in range(per_group):
            b = group * per_group + part
            rows = [c[b : b + 1] for c in coords]
            panel = jnp.concatenate([modes_ref[:, b * block : (b + 1) * block].astype(F32), *rows, pad], axis=0)
            place_row = place[b : b + 1]
            left = jnp.concatenate(
                [jnp.where(place_row == p, panel, 0.0).astype(BF16) for p in range(sites)], axis=0
            )
            right = (slot_iota == rank[b : b + 1]).astype(F32).astype(BF16)
            product = lax.dot_general(left, right, NT, preferred_element_type=F32)
            total = product if total is None else total + product
        for p in range(sites):
            piece = total[p * PANEL : (p + 1) * PANEL].astype(BF16)
            out_ref[p // 2, p % 2, :, group * slots : (group + 1) * slots] = piece


def bucket(owner, modes, meta):
    blocks, block = meta.shape
    owners = owner.shape[0] // 2
    slots = blocks * block // 8
    return pl.pallas_call(
        bucket_kernel,
        out_shape=jax.ShapeDtypeStruct((owners, 2, PANEL, slots), BF16),
        in_specs=[
            pl.BlockSpec(memory_space=pltpu.SMEM),
            pl.BlockSpec(memory_space=pltpu.VMEM),
            pl.BlockSpec(memory_space=pltpu.VMEM),
        ],
        out_specs=pl.BlockSpec(memory_space=pltpu.VMEM),
        compiler_params=pltpu.CompilerParams(vmem_limit_bytes=48 * 2**20),
        cost_estimate=pl.CostEstimate(flops=4 * 10**9, bytes_accessed=1500000, transcendentals=0),
    )(owner, modes, meta)


def fill_steps(panel_ref, trig_ref, left_ref, right_ref):
    width = panel_ref.shape[1]

    def lookup():
        cells = panel_ref[16:32].astype(F32)
        rows = lax.broadcasted_iota(I32, (24, width), 0).astype(F32)
        waves = [
            (jnp.where(rows < HALF, rows, rows - 11.0), jnp.where(rows < HALF, 0.25, 0.0)),
            (rows, 0.25),
            (rows, 0.0),
            (jnp.where(rows < HALF, rows, rows - 12.0), jnp.where(rows < HALF, 0.25, 0.0)),
        ]
        for part, axis in enumerate((0, 1, 1, 2)):
            wave, shift = waves[part]
            turn = wave * (cells[8 + axis : 9 + axis] * (1.0 / EDGE)) + shift
            trig_ref[24 * part : 24 * part + 24] = sine(turn - jnp.round(turn))

    def left(pair):
        values = panel_ref[...].astype(F32)[:24]
        first = values * trig_ref[2 * pair : 2 * pair + 1]
        if pair < HALF - 1:
            second = values * trig_ref[2 * pair + 1 : 2 * pair + 2]
        else:
            second = jnp.zeros((8, width), F32)
        both = jnp.concatenate([first, second], axis=0).astype(BF16)
        left_ref[48 * pair : 48 * pair + both.shape[0]] = both

    def right(pair):
        cos1, sin1 = trig_ref[24:48], trig_ref[48:72]
        cos_parts, sin_parts = [], []
        for wave in (2 * pair, 2 * pair + 1):
            cos2, sin2 = trig_ref[72 + wave : 73 + wave], trig_ref[84 + wave : 85 + wave]
            cos_parts.append(cos1 * cos2 - sin1 * sin2)
            sin_parts.append(sin1 * cos2 + cos1 * sin2)
        right_ref[48 * pair : 48 * pair + 48] = jnp.concatenate(cos_parts, axis=0).astype(BF16)
        right_ref[LANES + 48 * pair : LANES + 48 * pair + 48] = jnp.concatenate(sin_parts, axis=0).astype(BF16)

    steps = [lookup]
    for pair in range(HALF):
        steps.append(functools.partial(left, pair))
        if pair % 2:
            steps.append(functools.partial(right, pair // 2))
    return steps


def project_kernel(norm, panel_ref, wave_ref, out_ref, trig_ref, left0, left1, right0, right1, acc_ref, power_ref):
    lefts, rights = (left0, left1), (right0, right1)
    sources, places = panel_ref.shape[:2]
    for right in rights:
        right[288:LANES] = jnp.zeros((LANES - 288, right.shape[1]), BF16)
        right[LANES + 288 :] = jnp.zeros((LANES - 288, right.shape[1]), BF16)
    dests, width = wave_ref.shape
    first, second, third = split_flat(wave_ref[...].astype(F32))
    flip0 = first > HALF - 1
    flip2 = third > HALF - 1
    wave0 = jnp.where(flip0, EDGE - first, first)
    wave1 = jnp.where(flip2 & (second > 0), EDGE - second, second)
    wave2 = jnp.where(flip2, EDGE - third, third)
    column = wave2 * 24.0 + wave1
    group = wave0 * 2.0 + (flip0 != flip2).astype(F32)
    row_iota = lax.broadcasted_iota(I32, (LANES, width), 0).astype(F32)
    scale = 1.0 / norm

    def steps_of(chunk):
        slot = chunk % 2
        piece = panel_ref.at[chunk % sources, chunk // sources]
        return fill_steps(piece, trig_ref.at[slot], lefts[slot], rights[slot])

    def square():
        for wave in range(HALF):
            cc = acc_ref[24 * wave : 24 * wave + 24, :LANES]
            cs = acc_ref[24 * wave : 24 * wave + 24, LANES:]
            if wave:
                sc = acc_ref[24 * (11 + wave) : 24 * (12 + wave), :LANES]
                ss = acc_ref[24 * (11 + wave) : 24 * (12 + wave), LANES:]
                same = ((cc - ss) ** 2 + (cs + sc) ** 2) * scale
                other = ((cc + ss) ** 2 + (cs - sc) ** 2) * scale
            else:
                same = other = (cc**2 + cs**2) * scale
            power_ref[48 * wave : 48 * wave + 48] = jnp.concatenate([same, other], axis=0).astype(BF16)

    def pick(dest):
        chosen = (row_iota == column[dest : dest + 1]).astype(F32).astype(BF16)
        return jnp.dot(power_ref[...], chosen, preferred_element_type=F32)

    def store(place, dest, picked):
        total = jnp.zeros((24, width), F32)
        for g in range(2 * HALF):
            total += jnp.where(group[dest : dest + 1] == g, picked[24 * g : 24 * g + 24], 0.0)
        out_ref[dest, place] = total.astype(BF16)

    chunks = places * sources
    for step in steps_of(0):
        step()
    for chunk in range(chunks):
        slot = chunk % 2
        ahead = steps_of(chunk + 1) if chunk + 1 < chunks else []
        product = lax.dot_general(lefts[slot][...], rights[slot][...], NT, preferred_element_type=F32)
        for step in ahead:
            step()
        if chunk % sources == 0:
            acc_ref[...] = product
        else:
            acc_ref[...] += product
        if (chunk + 1) % sources == 0:
            place = chunk // sources
            square()
            picked = pick(0)
            for dest in range(dests):
                following = pick(dest + 1) if dest + 1 < dests else None
                store(place, dest, picked)
                picked = following


def project(panel, waves, norm):
    sources, places, rows, slots = panel.shape
    return pl.pallas_call(
        functools.partial(project_kernel, norm),
        out_shape=jax.ShapeDtypeStruct((waves.shape[0], places, 24, waves.shape[1]), BF16),
        in_specs=[pl.BlockSpec(memory_space=pltpu.VMEM)] * 2,
        out_specs=pl.BlockSpec(memory_space=pltpu.VMEM),
        scratch_shapes=[
            pltpu.VMEM((2, 96, slots), F32),
            pltpu.VMEM((ROWS_LHS, slots), BF16),
            pltpu.VMEM((ROWS_LHS, slots), BF16),
            pltpu.VMEM((2 * LANES, slots), BF16),
            pltpu.VMEM((2 * LANES, slots), BF16),
            pltpu.VMEM((ROWS_LHS, 2 * LANES), F32),
            pltpu.VMEM((576, LANES), BF16),
        ],
        compiler_params=pltpu.CompilerParams(vmem_limit_bytes=48 * 2**20),
        cost_estimate=pl.CostEstimate(flops=18 * 10**9, bytes_accessed=2000000, transcendentals=0),
    )(panel, waves)


def body(modes, atom_site, site_owner, translation, wavevectors):
    col_count = lax.axis_size("col")
    sites = site_owner.shape[0]
    atoms = translation.shape[0]
    norm = 3.0 * atoms * col_count / 2.0
    packed = jnp.concatenate([atom_site[:, 0] * 2**CELL_BITS + translation, wavevectors])
    packed = jnp.broadcast_to(packed[None], (col_count, packed.shape[0]))
    gathered = lax.all_to_all(packed, "col", split_axis=0, concat_axis=0, tiled=True)
    meta, waves = gathered[:, :atoms], gathered[:, atoms:]
    buckets = bucket(site_owner, modes, meta)
    panel = lax.all_to_all(buckets, "row", split_axis=0, concat_axis=0, tiled=True)
    power = project(panel, waves, norm)
    arrived = lax.all_to_all(power, "col", split_axis=0, concat_axis=0, tiled=True)
    arrived = arrived.transpose(1, 0, 2, 3).reshape(2, 3, -1, wavevectors.shape[0])
    projected = jnp.sum(arrived.astype(F32), axis=1)
    local = jnp.sum(projected, axis=0).reshape(lax.axis_size("row"), -1, wavevectors.shape[0])
    shares = lax.all_to_all(local, "row", split_axis=0, concat_axis=0, tiled=True)
    return projected, jnp.sum(shares, axis=0) * (1.0 / sites)


def solution(mesh):
    placed = (P("col", "row"), P(("row", "col"), None), P(), P(("row", "col")), P("col"))
    return jax.shard_map(
        body,
        mesh=mesh,
        in_specs=placed,
        out_specs=(P("row", None, "col"), P("row", "col")),
        check_vma=False,
    )
```

```python
import functools
import math

import jax
import jax.numpy as jnp
import numpy as np
from jax import lax
from jax.experimental import pallas as pl
from jax.experimental.pallas import tpu as pltpu
from jax.sharding import PartitionSpec as P

EDGE = 23
HALF = 12
F32, BF16, I32 = jnp.float32, jnp.bfloat16, jnp.int32
CELL_BITS = 14
PANEL = 32
SLOTS = 1024
STRIDE = 3 * SLOTS + 3 * SLOTS // 8
GROUP = 2048
ROWS_LHS = 560
MAIN = 256
SIDE = 48
SIDE_GROUPS = 10
COARSE = (0, 5, 16, 10, 21)
FINE = (0, 1, 12, 2, 13)
ORDER = COARSE + tuple(row for row in range(EDGE) if row not in COARSE)
NT = (((1,), (1,)), ((), ()))


def split_flat(flat):
    first = jnp.floor((flat + 0.5) * (1.0 / (EDGE * EDGE)))
    rest = flat - first * (EDGE * EDGE)
    second = jnp.floor((rest + 0.5) * (1.0 / EDGE))
    return first, second, rest - second * EDGE


def sine_terms():
    nodes = 0.25 * np.cos(np.pi * (np.arange(400) + 0.5) / 800.0)
    turn = 2.0 * nodes
    return [float(c) for c in np.polyfit(turn**2, np.sin(2.0 * np.pi * turn) / turn, 6)]


SINE = sine_terms()


def sine(turn):
    square = turn * turn
    total = SINE[0]
    for term in SINE[1:]:
        total = total * square + term
    return total * turn


def bucket_kernel(sites, block, modes_hbm, meta_ref, out_ref, modes_ref, cell_ref, copied):
    copy = pltpu.make_async_copy(modes_hbm, modes_ref, copied)
    copy.start()
    blocks = meta_ref.shape[0]
    owner_row = meta_ref[0:1, meta_ref.shape[1] - 128 :][:, :sites]
    down = lax.broadcasted_iota(I32, (sites, sites), 0)
    along = lax.broadcasted_iota(I32, (sites, sites), 1)
    owner = jnp.sum(jnp.where(down == along, owner_row, 0), axis=1, keepdims=True)
    same_owner = (owner == owner_row) & (along < down)
    order = (owner * 2 + jnp.sum(same_owner.astype(I32), axis=1, keepdims=True)).astype(F32)
    meta = meta_ref[:, :block]
    site = lax.shift_right_logical(meta, CELL_BITS)
    coords = split_flat((meta & (2**CELL_BITS - 1)).astype(F32))
    hot = [(site == s).astype(F32) for s in range(sites)]
    stacked = jnp.concatenate(hot, axis=0).astype(BF16)
    source = lax.broadcasted_iota(I32, (block, block), 0)
    target = lax.broadcasted_iota(I32, (block, block), 1)
    earlier = (source < target).astype(F32).astype(BF16)
    before = jnp.dot(stacked, earlier, preferred_element_type=F32)
    per_group = GROUP // block
    upper = lax.broadcasted_iota(I32, (sites * blocks, sites * blocks), 0)
    lower = lax.broadcasted_iota(I32, (sites * blocks, sites * blocks), 1)
    same = (upper // per_group == lower // per_group) & (lower < upper)
    offsets = jnp.sum(
        jnp.dot(same.astype(F32).astype(BF16), stacked, preferred_element_type=F32), axis=1, keepdims=True
    )
    before = before + offsets
    rank = jnp.zeros(meta.shape, F32)
    place = jnp.zeros(meta.shape, F32)
    for s in range(sites):
        rank += hot[s] * before[s * blocks : (s + 1) * blocks]
        place += hot[s] * order[s : s + 1]
    copy.wait()
    slots = GROUP // 8
    slot_iota = lax.broadcasted_iota(I32, (slots, block), 0).astype(F32)
    pad = jnp.zeros((5, block), F32)
    for group in range(blocks // per_group):
        total = None
        for part in range(per_group):
            b = group * per_group + part
            rows = [c[b : b + 1] for c in coords]
            panel = jnp.concatenate([modes_ref[:, b * block : (b + 1) * block].astype(F32), *rows, pad], axis=0)
            place_row = place[b : b + 1]
            left = jnp.concatenate(
                [jnp.where(place_row == p, panel, 0.0).astype(BF16) for p in range(sites)], axis=0
            )
            right = (slot_iota == rank[b : b + 1]).astype(F32).astype(BF16)
            product = lax.dot_general(left, right, NT, preferred_element_type=F32)
            total = product if total is None else total + product
        for p in range(sites):
            start = (p % 2) * STRIDE + group * slots
            for part in range(3):
                piece = total[p * PANEL + 8 * part : p * PANEL + 8 * part + 8].astype(BF16)
                out_ref[p // 2, :, start + part * SLOTS : start + part * SLOTS + slots] = piece
            for half in range(slots // 128):
                row = group * (slots // 128) + half
                for axis in range(3):
                    line = total[p * PANEL + 24 + axis : p * PANEL + 25 + axis, 128 * half : 128 * half + 128]
                    cell_ref[p, row : row + 1, 128 * axis : 128 * axis + 128] = line
    for p in range(sites):
        start = (p % 2) * STRIDE + 3 * SLOTS
        out_ref[p // 2, :, start : start + 384] = cell_ref[p].astype(BF16)


def bucket(modes, meta, sites, block):
    rows, atoms = modes.shape
    return pl.pallas_call(
        functools.partial(bucket_kernel, sites, block),
        out_shape=jax.ShapeDtypeStruct((sites // 2, 8, 2 * STRIDE), BF16),
        in_specs=[pl.BlockSpec(memory_space=pl.ANY), pl.BlockSpec(memory_space=pltpu.VMEM)],
        out_specs=pl.BlockSpec(memory_space=pltpu.VMEM),
        scratch_shapes=[
            pltpu.VMEM((rows, atoms), BF16),
            pltpu.VMEM((sites, 8, 384), F32),
            pltpu.SemaphoreType.DMA(()),
        ],
        compiler_params=pltpu.CompilerParams(vmem_limit_bytes=48 * 2**20),
        cost_estimate=pl.CostEstimate(flops=4 * 10**9, bytes_accessed=1500000, transcendentals=0),
    )(modes, meta)


def fill_steps(panel_ref, base, trig_ref, left_ref, right_ref):
    width = SLOTS

    def lookup():
        lines = panel_ref[:, base + 3 * SLOTS : base + STRIDE].astype(F32)
        cells = [
            jnp.concatenate([lines[row : row + 1, 128 * axis : 128 * axis + 128] for row in range(8)], axis=1)
            for axis in range(3)
        ]
        rows = lax.broadcasted_iota(I32, (24, width), 0).astype(F32)
        waves = [
            (jnp.where(rows < HALF, rows, rows - 11.0), jnp.where(rows < HALF, 0.25, 0.0)),
            (rows, 0.25),
            (rows, 0.0),
            (jnp.where(rows < HALF, rows, rows - 12.0), jnp.where(rows < HALF, 0.25, 0.0)),
        ]
        for part, axis in enumerate((0, 1, 1, 2)):
            wave, shift = waves[part]
            turn = wave * (cells[axis] * (1.0 / EDGE)) + shift
            trig_ref[24 * part : 24 * part + 24] = sine(turn - jnp.round(turn))

    def left(pair):
        values = jnp.concatenate(
            [panel_ref[:, base + SLOTS * part : base + SLOTS * part + SLOTS].astype(F32) for part in range(3)], axis=0
        )
        row = ORDER[2 * pair]
        first = values * trig_ref[row : row + 1]
        if pair < HALF - 1:
            row = ORDER[2 * pair + 1]
            second = values * trig_ref[row : row + 1]
        else:
            second = jnp.zeros((8, width), F32)
        both = jnp.concatenate([first, second], axis=0).astype(BF16)
        left_ref[48 * pair : 48 * pair + both.shape[0]] = both

    def plane(wave, low, high):
        cos1, sin1 = trig_ref[24 + low : 24 + high], trig_ref[48 + low : 48 + high]
        cos2, sin2 = trig_ref[72 + wave : 73 + wave], trig_ref[84 + wave : 85 + wave]
        return cos1 * cos2 - sin1 * sin2, sin1 * cos2 + cos1 * sin2

    def right(pair):
        parts = [plane(wave, 0, 24) for wave in (2 * pair + 1, 2 * pair + 2)]
        for part in range(2):
            both = jnp.concatenate([parts[0][part], parts[1][part]], axis=0).astype(BF16)
            right_ref[MAIN * part + 48 * pair : MAIN * part + 48 * pair + 48] = both

    def right_last():
        parts = plane(HALF - 1, 0, 16)
        for part in range(2):
            right_ref[MAIN * part + 240 : MAIN * part + 256] = parts[part].astype(BF16)

    def side():
        cos, sin = plane(HALF - 1, 16, 24)
        base = jnp.concatenate([trig_ref[24:40], cos, trig_ref[48:64], sin], axis=0)
        for block, row in enumerate(FINE):
            start = 2 * MAIN + SIDE * block
            right_ref[start : start + SIDE] = (base * trig_ref[row : row + 1]).astype(BF16)

    steps = [lookup] + [functools.partial(left, pair) for pair in range(HALF)]
    return steps + [functools.partial(right, pair) for pair in range(5)] + [right_last, side]


def project_kernel(
    norm, panel_ref, wave_ref, out_ref, trig_ref, left0, left1, right0, right1, acc_ref, side_ref, power_ref
):
    lefts, rights = (left0, left1), (right0, right1)
    sources, places = panel_ref.shape[0], 2
    for right in rights:
        right[2 * MAIN + 5 * SIDE :] = jnp.zeros((256 - 5 * SIDE, right.shape[1]), BF16)
    dests = out_ref.shape[0]
    width = out_ref.shape[3]
    first, second, third = split_flat(wave_ref[...].astype(F32))
    flip0 = first > HALF - 1
    flip12 = (third > HALF - 1) | ((third == 0) & (second > HALF - 1))
    wave0 = jnp.where(flip0, EDGE - first, first)
    wave1 = jnp.where(flip12 & (second > 0), EDGE - second, second)
    wave2 = jnp.where(flip12 & (third > 0), EDGE - third, third)
    group = wave0 * 2.0 + (flip0 != flip12).astype(F32)
    side_row = (group >= SIDE_GROUPS).astype(F32) + (group >= 2 * SIDE_GROUPS).astype(F32)
    in_side = (wave2 == 0) | ((wave2 == HALF - 1) & (wave1 > 15))
    column = jnp.where(in_side, (group - SIDE_GROUPS * side_row) * 24.0, (wave2 - 1.0) * 24.0) + wave1
    group = jnp.where(in_side, 2.0 * HALF + side_row, group)
    row_iota = lax.broadcasted_iota(I32, (MAIN, width), 0).astype(F32)
    lane_iota = lax.broadcasted_iota(I32, (24, 256), 1)
    scale = 1.0 / norm

    def steps_of(chunk):
        slot = chunk % 2
        base = chunk // sources * STRIDE
        return fill_steps(panel_ref.at[chunk % sources], base, trig_ref.at[slot], lefts[slot], rights[slot])

    def powers(cc, cs, sc, ss):
        return ((cc - ss) ** 2 + (cs + sc) ** 2) * scale, ((cc + ss) ** 2 + (cs - sc) ** 2) * scale

    def square():
        for wave in range(HALF):
            start = 24 * ORDER.index(wave)
            cc, cs = acc_ref[start : start + 24, :MAIN], acc_ref[start : start + 24, MAIN:]
            sc = ss = jnp.zeros_like(cc)
            if wave:
                start = 24 * ORDER.index(11 + wave)
                sc, ss = acc_ref[start : start + 24, :MAIN], acc_ref[start : start + 24, MAIN:]
            power_ref[48 * wave : 48 * wave + 48] = jnp.concatenate(powers(cc, cs, sc, ss), axis=0).astype(BF16)

    def square_side():
        blocks = []
        for row in range(5):
            whole = side_ref[24 * row : 24 * row + 24]
            shifted = [whole] + [pltpu.roll(whole, 256 - SIDE * block, 1) for block in range(1, 5)]
            blocks.append([piece[:, :128] for piece in shifted])
        packed = [jnp.zeros((24, 256), F32) for _ in range(3)]
        for wave in range(HALF):
            coarse = (wave + 2) // 5
            fine = wave - 5 * coarse
            far, near, sign = 2 * coarse, 2 * abs(fine), 1.0 if fine > 0 else -1.0
            if not coarse:
                cos = blocks[0][max(near - 1, 0)]
                sin = blocks[0][near] if near else jnp.zeros_like(cos)
            elif not fine:
                cos, sin = blocks[far - 1][0], blocks[far][0]
            else:
                cos = blocks[far - 1][near - 1] - sign * blocks[far][near]
                sin = blocks[far][near - 1] + sign * blocks[far - 1][near]
            both = powers(cos, pltpu.roll(cos, 128 - 24, 1), sin, pltpu.roll(sin, 128 - 24, 1))
            for flipped in range(2):
                index = 2 * wave + flipped
                wide = jnp.concatenate([both[flipped], jnp.zeros((24, 128), F32)], axis=1)
                wide = jnp.where(lane_iota < 24, wide, 0.0)
                at = 24 * (index % SIDE_GROUPS)
                packed[index // SIDE_GROUPS] += pltpu.roll(wide, at, 1) if at else wide
        rows = jnp.concatenate(packed + [jnp.zeros((8, 256), F32)], axis=0)
        power_ref[576:656] = rows.astype(BF16)

    def pick(dest):
        chosen = (row_iota == column[dest : dest + 1]).astype(F32).astype(BF16)
        return jnp.dot(power_ref[...], chosen, preferred_element_type=F32)

    def store(place, dest, picked):
        total = jnp.zeros((24, width), F32)
        for g in range(2 * HALF + 3):
            total += jnp.where(group[dest : dest + 1] == g, picked[24 * g : 24 * g + 24], 0.0)
        out_ref[dest, place] = total.astype(BF16)

    chunks = places * sources
    for step in steps_of(0):
        step()
    for chunk in range(chunks):
        slot = chunk % 2
        left, right = lefts[slot], rights[slot]
        product = lax.dot_general(left[...], right[: 2 * MAIN], NT, preferred_element_type=F32)
        side = lax.dot_general(left[:128], right[2 * MAIN :], NT, preferred_element_type=F32)
        for step in steps_of(chunk + 1) if chunk + 1 < chunks else []:
            step()
        if chunk % sources == 0:
            acc_ref[...] = product
            side_ref[...] = side
        else:
            acc_ref[...] += product
            side_ref[...] += side
        if (chunk + 1) % sources == 0:
            place = chunk // sources
            square()
            square_side()
            picked = pick(0)
            for dest in range(dests):
                following = pick(dest + 1) if dest + 1 < dests else None
                store(place, dest, picked)
                picked = following


def project(panel, waves, norm):
    places, slots = 2, SLOTS
    return pl.pallas_call(
        functools.partial(project_kernel, norm),
        out_shape=jax.ShapeDtypeStruct((waves.shape[0], places, 24, waves.shape[1]), BF16),
        in_specs=[pl.BlockSpec(memory_space=pltpu.VMEM)] * 2,
        out_specs=pl.BlockSpec(memory_space=pltpu.VMEM),
        scratch_shapes=[
            pltpu.VMEM((2, 96, slots), F32),
            pltpu.VMEM((ROWS_LHS, slots), BF16),
            pltpu.VMEM((ROWS_LHS, slots), BF16),
            pltpu.VMEM((2 * MAIN + 256, slots), BF16),
            pltpu.VMEM((2 * MAIN + 256, slots), BF16),
            pltpu.VMEM((ROWS_LHS, 2 * MAIN), F32),
            pltpu.VMEM((128, 256), F32),
            pltpu.VMEM((656, MAIN), BF16),
        ],
        compiler_params=pltpu.CompilerParams(vmem_limit_bytes=48 * 2**20),
        cost_estimate=pl.CostEstimate(flops=18 * 10**9, bytes_accessed=2000000, transcendentals=0),
    )(panel, waves)


def body(modes, atom_site, site_owner, translation, wavevectors):
    col_count = lax.axis_size("col")
    sites = site_owner.shape[0]
    atoms = translation.shape[0]
    norm = 3.0 * atoms * col_count / 2.0
    message = [
        atom_site[:, 0] * 2**CELL_BITS + translation,
        wavevectors,
        jnp.pad(site_owner, (0, 128 - sites)),
    ]
    packed = jnp.concatenate(message)
    packed = jnp.broadcast_to(packed[None], (col_count, packed.shape[0]))
    meta = lax.all_to_all(packed, "col", split_axis=0, concat_axis=0, tiled=True)
    waves = meta[:, atoms : atoms + wavevectors.shape[0]]
    buckets = bucket(modes, meta, sites, atoms)
    panel = lax.all_to_all(buckets, "row", split_axis=0, concat_axis=0, tiled=True)
    power = project(panel, waves, norm)
    arrived = lax.all_to_all(power, "col", split_axis=0, concat_axis=0, tiled=True)
    arrived = arrived.transpose(1, 0, 2, 3).reshape(2, 3, -1, wavevectors.shape[0])
    projected = jnp.sum(arrived.astype(F32), axis=1)
    local = jnp.sum(projected, axis=0).reshape(lax.axis_size("row"), -1, wavevectors.shape[0])
    shares = lax.all_to_all(local, "row", split_axis=0, concat_axis=0, tiled=True)
    return projected, jnp.sum(shares, axis=0) * (1.0 / sites)


def solution(mesh):
    placed = (P("col", "row"), P(("row", "col"), None), P(), P(("row", "col")), P("col"))
    return jax.shard_map(
        body,
        mesh=mesh,
        in_specs=placed,
        out_specs=(P("row", None, "col"), P("row", "col")),
        check_vma=False,
    )
```

```python
import functools
import math

import jax
import jax.numpy as jnp
import numpy as np
from jax import lax
from jax.experimental import pallas as pl
from jax.experimental.pallas import tpu as pltpu
from jax.sharding import PartitionSpec as P

EDGE = 23
HALF = 12
F32, BF16, I32 = jnp.float32, jnp.bfloat16, jnp.int32
CELL_BITS = 14
PANEL = 32
SLOTS = 1024
STRIDE = 3 * SLOTS + 3 * SLOTS // 8
CAPACITY = 64
ROWS_LHS = 560
MAIN = 256
SIDE = 48
SIDE_GROUPS = 10
COARSE = (0, 5, 16, 10, 21)
FINE = (0, 1, 12, 2, 13)
ORDER = COARSE + tuple(row for row in range(EDGE) if row not in COARSE)
NT = (((1,), (1,)), ((), ()))


def split_flat(flat):
    first = jnp.floor((flat + 0.5) * (1.0 / (EDGE * EDGE)))
    rest = flat - first * (EDGE * EDGE)
    second = jnp.floor((rest + 0.5) * (1.0 / EDGE))
    return first, second, rest - second * EDGE


def turn_terms(function, odd, count):
    turn = 0.5 * np.cos(np.pi * (np.arange(400) + 0.5) / 800.0)
    values = function(2.0 * np.pi * turn) / (turn if odd else 1.0)
    return [float(c) for c in np.polyfit(turn**2, values, count - 1)]


SINE = turn_terms(np.sin, True, 6)
COSINE = turn_terms(np.cos, False, 7)


def horner(terms, square):
    total = terms[0]
    for term in terms[1:]:
        total = total * square + term
    return total


def bucket_kernel(sites, block, modes_ref, meta_ref, out_ref, cell_ref):
    blocks = meta_ref.shape[0]
    owner_row = meta_ref[0:1, meta_ref.shape[1] - 128 :][:, :sites]
    down = lax.broadcasted_iota(I32, (sites, sites), 0)
    along = lax.broadcasted_iota(I32, (sites, sites), 1)
    owner = jnp.sum(jnp.where(down == along, owner_row, 0), axis=1, keepdims=True)
    same_owner = (owner == owner_row) & (along < down)
    order = (owner * 2 + jnp.sum(same_owner.astype(I32), axis=1, keepdims=True)).astype(F32)
    meta = meta_ref[:, :block]
    site = lax.shift_right_logical(meta, CELL_BITS)
    coords = split_flat((meta & (2**CELL_BITS - 1)).astype(F32))
    hot = [(site == s).astype(F32) for s in range(sites)]
    stacked = jnp.concatenate(hot, axis=0).astype(BF16)
    source = lax.broadcasted_iota(I32, (block, block), 0)
    target = lax.broadcasted_iota(I32, (block, block), 1)
    earlier = (source < target).astype(F32).astype(BF16)
    before = jnp.dot(stacked, earlier, preferred_element_type=F32)
    rank = jnp.zeros(meta.shape, F32)
    place = jnp.zeros(meta.shape, F32)
    for s in range(sites):
        rank += hot[s] * before[s * blocks : (s + 1) * blocks]
        place += hot[s] * order[s : s + 1]
    quarter = jnp.floor(place * 0.25)
    column = (place - 4.0 * quarter) * CAPACITY + rank
    slots = 4 * CAPACITY
    slot_iota = lax.broadcasted_iota(I32, (slots, block), 0).astype(F32)
    low_lanes = lax.broadcasted_iota(I32, (PANEL, 128), 1) < CAPACITY
    pad = jnp.zeros((5, block), F32)

    def sort_block(b):
        rows = [c[b : b + 1] for c in coords]
        panel = jnp.concatenate([modes_ref[:, b * block : (b + 1) * block].astype(F32), *rows, pad], axis=0)
        row = quarter[b : b + 1]
        left = jnp.concatenate([jnp.where(row == q, panel, 0.0).astype(BF16) for q in range(sites // 4)], axis=0)
        right = (slot_iota == column[b : b + 1]).astype(F32).astype(BF16)
        return lax.dot_general(left, right, NT, preferred_element_type=F32)

    for pair in range(blocks // 2):
        even, odd = sort_block(2 * pair), sort_block(2 * pair + 1)
        for p in range(sites):
            rows = slice((p // 4) * PANEL, (p // 4) * PANEL + PANEL)
            lanes = slice((p % 4) // 2 * 128, (p % 4) // 2 * 128 + 128)
            low, high = even[rows, lanes], odd[rows, lanes]
            if p % 2:
                low = pltpu.roll(low, CAPACITY, 1)
            else:
                high = pltpu.roll(high, CAPACITY, 1)
            total = jnp.where(low_lanes, low, high)
            start = (p % 2) * STRIDE + 128 * pair
            for part in range(3):
                piece = total[8 * part : 8 * part + 8].astype(BF16)
                out_ref[p // 2, :, start + part * SLOTS : start + part * SLOTS + 128] = piece
            for axis in range(3):
                cell_ref[p, pair : pair + 1, 128 * axis : 128 * axis + 128] = total[24 + axis : 25 + axis]
    for p in range(sites):
        start = (p % 2) * STRIDE + 3 * SLOTS
        out_ref[p // 2, :, start : start + 384] = cell_ref[p].astype(BF16)


def bucket(modes, meta, sites, block):
    return pl.pallas_call(
        functools.partial(bucket_kernel, sites, block),
        out_shape=jax.ShapeDtypeStruct((sites // 2, 8, 2 * STRIDE), BF16),
        in_specs=[pl.BlockSpec(memory_space=pltpu.VMEM)] * 2,
        out_specs=pl.BlockSpec(memory_space=pltpu.VMEM),
        scratch_shapes=[pltpu.VMEM((sites, 8, 384), F32)],
        compiler_params=pltpu.CompilerParams(vmem_limit_bytes=48 * 2**20),
        cost_estimate=pl.CostEstimate(flops=4 * 10**9, bytes_accessed=1500000, transcendentals=0),
    )(modes, meta)


def table_row(row):
    return row if row < HALF else row + 1


def fill_steps(panel_ref, base, trig_ref, left_ref, right_ref):
    width = SLOTS
    loaded = []

    def lookup():
        lines = panel_ref[:, base + 3 * SLOTS : base + STRIDE].astype(F32)
        cells = [
            jnp.concatenate([lines[row : row + 1, 128 * axis : 128 * axis + 128] for row in range(8)], axis=1)
            for axis in range(3)
        ]
        rows = lax.broadcasted_iota(I32, (24, width), 0).astype(F32)
        starts = ((0, 12, 16), (24, 48, 24), (72, 88, 16))
        for axis, (cos_start, sin_start, count) in enumerate(starts):
            turn = rows[:count] * (cells[axis] * (1.0 / EDGE))
            turn = turn - jnp.round(turn)
            square = turn * turn
            cos, sin = horner(COSINE, square), horner(SINE, square) * turn
            if axis == 0:
                cos, sin = cos[:HALF], sin[:HALF]
            trig_ref[cos_start : cos_start + cos.shape[0]] = cos
            trig_ref[sin_start : sin_start + sin.shape[0]] = sin

    def left(pair):
        if not loaded:
            parts = [panel_ref[:, base + SLOTS * part : base + SLOTS * part + SLOTS] for part in range(3)]
            loaded.append(jnp.concatenate([part.astype(F32) for part in parts], axis=0))
        values = loaded[0]
        row = table_row(ORDER[2 * pair])
        first = values * trig_ref[row : row + 1]
        if pair < HALF - 1:
            row = table_row(ORDER[2 * pair + 1])
            second = values * trig_ref[row : row + 1]
        else:
            second = jnp.zeros((8, width), F32)
        both = jnp.concatenate([first, second], axis=0).astype(BF16)
        left_ref[48 * pair : 48 * pair + both.shape[0]] = both

    def plane(wave, low, high):
        cos1, sin1 = trig_ref[24 + low : 24 + high], trig_ref[48 + low : 48 + high]
        cos2, sin2 = trig_ref[72 + wave : 73 + wave], trig_ref[88 + wave : 89 + wave]
        return cos1 * cos2 - sin1 * sin2, sin1 * cos2 + cos1 * sin2

    def right(pair):
        parts = [plane(wave, 0, 24) for wave in (2 * pair + 1, 2 * pair + 2)]
        for part in range(2):
            both = jnp.concatenate([parts[0][part], parts[1][part]], axis=0).astype(BF16)
            right_ref[MAIN * part + 48 * pair : MAIN * part + 48 * pair + 48] = both

    def right_last():
        parts = plane(HALF - 1, 0, 16)
        for part in range(2):
            right_ref[MAIN * part + 240 : MAIN * part + 256] = parts[part].astype(BF16)

    def side():
        cos, sin = plane(HALF - 1, 16, 24)
        base = jnp.concatenate([trig_ref[24:40], cos, trig_ref[48:64], sin], axis=0)
        for block, row in enumerate(map(table_row, FINE)):
            start = 2 * MAIN + SIDE * block
            right_ref[start : start + SIDE] = (base * trig_ref[row : row + 1]).astype(BF16)

    steps = [lookup] + [functools.partial(left, pair) for pair in range(HALF)]
    return steps + [functools.partial(right, pair) for pair in range(5)] + [right_last, side]


def project_kernel(
    norm, panel_ref, wave_ref, out_ref, trig_ref, left0, left1, right0, right1, acc_ref, side_ref, power_ref
):
    lefts, rights = (left0, left1), (right0, right1)
    sources, places = panel_ref.shape[0], 2
    for right in rights:
        right[2 * MAIN + 5 * SIDE :] = jnp.zeros((256 - 5 * SIDE, right.shape[1]), BF16)
    dests = out_ref.shape[0]
    width = out_ref.shape[3]
    first, second, third = split_flat(wave_ref[...].astype(F32))
    flip0 = first > HALF - 1
    flip12 = (third > HALF - 1) | ((third == 0) & (second > HALF - 1))
    wave0 = jnp.where(flip0, EDGE - first, first)
    wave1 = jnp.where(flip12 & (second > 0), EDGE - second, second)
    wave2 = jnp.where(flip12 & (third > 0), EDGE - third, third)
    group = wave0 * 2.0 + (flip0 != flip12).astype(F32)
    side_row = (group >= SIDE_GROUPS).astype(F32) + (group >= 2 * SIDE_GROUPS).astype(F32)
    in_side = (wave2 == 0) | ((wave2 == HALF - 1) & (wave1 > 15))
    column = jnp.where(in_side, (group - SIDE_GROUPS * side_row) * 24.0, (wave2 - 1.0) * 24.0) + wave1
    group = jnp.where(in_side, 2.0 * HALF + side_row, group)
    row_iota = lax.broadcasted_iota(I32, (MAIN, width), 0).astype(F32)
    lane_iota = lax.broadcasted_iota(I32, (24, 256), 1)
    scale = 1.0 / norm

    def steps_of(chunk):
        slot = chunk % 2
        base = chunk // sources * STRIDE
        return fill_steps(panel_ref.at[chunk % sources], base, trig_ref.at[slot], lefts[slot], rights[slot])

    def powers(cc, cs, sc, ss):
        return ((cc - ss) ** 2 + (cs + sc) ** 2) * scale, ((cc + ss) ** 2 + (cs - sc) ** 2) * scale

    def square(place):
        for wave in range(HALF):
            start = 24 * ORDER.index(wave)
            cc, cs = acc_ref[place, start : start + 24, :MAIN], acc_ref[place, start : start + 24, MAIN:]
            sc = ss = jnp.zeros_like(cc)
            if wave:
                start = 24 * ORDER.index(11 + wave)
                sc, ss = acc_ref[place, start : start + 24, :MAIN], acc_ref[place, start : start + 24, MAIN:]
            power_ref[48 * wave : 48 * wave + 48] = jnp.concatenate(powers(cc, cs, sc, ss), axis=0).astype(BF16)

    def square_side(place):
        blocks = []
        for row in range(5):
            whole = side_ref[place, 24 * row : 24 * row + 24]
            shifted = [whole] + [pltpu.roll(whole, 256 - SIDE * block, 1) for block in range(1, 5)]
            blocks.append([piece[:, :128] for piece in shifted])
        packed = [jnp.zeros((24, 256), F32) for _ in range(3)]
        for wave in range(HALF):
            coarse = (wave + 2) // 5
            fine = wave - 5 * coarse
            far, near, sign = 2 * coarse, 2 * abs(fine), 1.0 if fine > 0 else -1.0
            if not coarse:
                cos = blocks[0][max(near - 1, 0)]
                sin = blocks[0][near] if near else jnp.zeros_like(cos)
            elif not fine:
                cos, sin = blocks[far - 1][0], blocks[far][0]
            else:
                cos = blocks[far - 1][near - 1] - sign * blocks[far][near]
                sin = blocks[far][near - 1] + sign * blocks[far - 1][near]
            both = powers(cos, pltpu.roll(cos, 128 - 24, 1), sin, pltpu.roll(sin, 128 - 24, 1))
            for flipped in range(2):
                index = 2 * wave + flipped
                wide = jnp.concatenate([both[flipped], jnp.zeros((24, 128), F32)], axis=1)
                wide = jnp.where(lane_iota < 24, wide, 0.0)
                at = 24 * (index % SIDE_GROUPS)
                packed[index // SIDE_GROUPS] += pltpu.roll(wide, at, 1) if at else wide
        rows = jnp.concatenate(packed + [jnp.zeros((8, 256), F32)], axis=0)
        power_ref[576:656] = rows.astype(BF16)

    def pick(dest):
        chosen = (row_iota == column[dest : dest + 1]).astype(F32).astype(BF16)
        return jnp.dot(power_ref[...], chosen, preferred_element_type=F32)

    def store(place, dest, picked):
        total = jnp.zeros((24, width), F32)
        for g in range(2 * HALF + 3):
            total += jnp.where(group[dest : dest + 1] == g, picked[24 * g : 24 * g + 24], 0.0)
        out_ref[dest, place] = total.astype(BF16)

    def finish(place):
        square(place)
        square_side(place)
        picked = pick(0)
        for dest in range(dests):
            following = pick(dest + 1) if dest + 1 < dests else None
            store(place, dest, picked)
            picked = following

    chunks = places * sources
    for step in steps_of(0):
        step()
    for chunk in range(chunks):
        slot = chunk % 2
        left, right = lefts[slot], rights[slot]
        product = lax.dot_general(left[...], right[: 2 * MAIN], NT, preferred_element_type=F32)
        side = lax.dot_general(left[:128], right[2 * MAIN :], NT, preferred_element_type=F32)
        for step in steps_of(chunk + 1) if chunk + 1 < chunks else []:
            step()
        place = chunk // sources
        if chunk % sources == 0:
            acc_ref[place] = product
            side_ref[place] = side
        else:
            acc_ref[place] += product
            side_ref[place] += side
        if (chunk + 1) % sources == 0:
            finish(place)


def project(panel, waves, norm):
    places, slots = 2, SLOTS
    return pl.pallas_call(
        functools.partial(project_kernel, norm),
        out_shape=jax.ShapeDtypeStruct((waves.shape[0], places, 24, waves.shape[1]), BF16),
        in_specs=[pl.BlockSpec(memory_space=pltpu.VMEM)] * 2,
        out_specs=pl.BlockSpec(memory_space=pltpu.VMEM),
        scratch_shapes=[
            pltpu.VMEM((2, 104, slots), F32),
            pltpu.VMEM((ROWS_LHS, slots), BF16),
            pltpu.VMEM((ROWS_LHS, slots), BF16),
            pltpu.VMEM((2 * MAIN + 256, slots), BF16),
            pltpu.VMEM((2 * MAIN + 256, slots), BF16),
            pltpu.VMEM((places, ROWS_LHS, 2 * MAIN), F32),
            pltpu.VMEM((places, 128, 256), F32),
            pltpu.VMEM((656, MAIN), BF16),
        ],
        compiler_params=pltpu.CompilerParams(vmem_limit_bytes=48 * 2**20),
        cost_estimate=pl.CostEstimate(flops=18 * 10**9, bytes_accessed=2000000, transcendentals=0),
    )(panel, waves)


def body(modes, atom_site, site_owner, translation, wavevectors):
    col_count = lax.axis_size("col")
    sites = site_owner.shape[0]
    atoms = translation.shape[0]
    norm = 3.0 * atoms * col_count / 2.0
    message = [
        atom_site[:, 0] * 2**CELL_BITS + translation,
        wavevectors,
        jnp.pad(site_owner, (0, 128 - sites)),
    ]
    packed = jnp.concatenate(message)
    packed = jnp.broadcast_to(packed[None], (col_count, packed.shape[0]))
    meta = lax.all_to_all(packed, "col", split_axis=0, concat_axis=0, tiled=True)
    waves = meta[:, atoms : atoms + wavevectors.shape[0]]
    buckets = bucket(modes, meta, sites, atoms)
    panel = lax.all_to_all(buckets, "row", split_axis=0, concat_axis=0, tiled=True)
    power = project(panel, waves, norm)
    arrived = lax.all_to_all(power, "col", split_axis=0, concat_axis=0, tiled=True)
    arrived = arrived.transpose(1, 0, 2, 3).reshape(2, 3, -1, wavevectors.shape[0])
    projected = jnp.sum(arrived.astype(F32), axis=1)
    local = jnp.sum(projected, axis=0).reshape(lax.axis_size("row"), -1, wavevectors.shape[0])
    shares = lax.all_to_all(local, "row", split_axis=0, concat_axis=0, tiled=True)
    return projected, jnp.sum(shares, axis=0) * (1.0 / sites)


def solution(mesh):
    placed = (P("col", "row"), P(("row", "col"), None), P(), P(("row", "col")), P("col"))
    return jax.shard_map(
        body,
        mesh=mesh,
        in_specs=placed,
        out_specs=(P("row", None, "col"), P("row", "col")),
        check_vma=False,
    )
```

```python
import functools
import math

import jax
import jax.numpy as jnp
import numpy as np
from jax import lax
from jax.experimental import pallas as pl
from jax.experimental.pallas import tpu as pltpu
from jax.sharding import PartitionSpec as P

EDGE = 23
HALF = 12
F32, BF16, I32 = jnp.float32, jnp.bfloat16, jnp.int32
CELL_BITS = 14
PANEL = 32
SLOTS = 1024
STRIDE = 3 * SLOTS + 3 * SLOTS // 8
CAPACITY = 64
ROWS_LHS = 560
MAIN = 256
SIDE = 48
SIDE_GROUPS = 10
COARSE = (0, 5, 16, 10, 21)
FINE = (0, 1, 12, 2, 13)
ORDER = COARSE + tuple(row for row in range(EDGE) if row not in COARSE)
NT = (((1,), (1,)), ((), ()))


def split_flat(flat):
    first = jnp.floor((flat + 0.5) * (1.0 / (EDGE * EDGE)))
    rest = flat - first * (EDGE * EDGE)
    second = jnp.floor((rest + 0.5) * (1.0 / EDGE))
    return first, second, rest - second * EDGE


def turn_terms(function, odd, count):
    turn = 0.5 * np.cos(np.pi * (np.arange(400) + 0.5) / 800.0)
    values = function(2.0 * np.pi * turn) / (turn if odd else 1.0)
    return [float(c) for c in np.polyfit(turn**2, values, count - 1)]


SINE = turn_terms(np.sin, True, 6)
COSINE = turn_terms(np.cos, False, 7)


def horner(terms, square):
    total = terms[0]
    for term in terms[1:]:
        total = total * square + term
    return total


def rank_kernel(sites, block, meta_ref, plan_ref):
    blocks = meta_ref.shape[0]
    owner_row = meta_ref[0:1, meta_ref.shape[1] - 128 :][:, :sites]
    down = lax.broadcasted_iota(I32, (sites, sites), 0)
    along = lax.broadcasted_iota(I32, (sites, sites), 1)
    owner = jnp.sum(jnp.where(down == along, owner_row, 0), axis=1, keepdims=True)
    same_owner = (owner == owner_row) & (along < down)
    order = (owner * 2 + jnp.sum(same_owner.astype(I32), axis=1, keepdims=True)).astype(F32)
    meta = meta_ref[:, :block]
    site = lax.shift_right_logical(meta, CELL_BITS)
    coords = split_flat((meta & (2**CELL_BITS - 1)).astype(F32))
    hot = [(site == s).astype(F32) for s in range(sites)]
    stacked = jnp.concatenate(hot, axis=0).astype(BF16)
    source = lax.broadcasted_iota(I32, (block, block), 0)
    target = lax.broadcasted_iota(I32, (block, block), 1)
    earlier = (source < target).astype(F32).astype(BF16)
    before = jnp.dot(stacked, earlier, preferred_element_type=F32)
    rank = jnp.zeros(meta.shape, F32)
    place = jnp.zeros(meta.shape, F32)
    for s in range(sites):
        rank += hot[s] * before[s * blocks : (s + 1) * blocks]
        place += hot[s] * order[s : s + 1]
    quarter = jnp.floor(place * 0.25)
    column = (place - 4.0 * quarter) * CAPACITY + rank
    for row, values in enumerate((quarter, column, *coords)):
        plan_ref[row] = values


def bucket_kernel(modes_ref, plan_ref, out_ref, cell_ref):
    sites = cell_ref.shape[0]
    blocks, block = plan_ref.shape[1:]
    slots = 4 * CAPACITY
    slot_iota = lax.broadcasted_iota(I32, (slots, block), 0).astype(F32)
    low_lanes = lax.broadcasted_iota(I32, (PANEL, 128), 1) < CAPACITY
    pad = jnp.zeros((5, block), F32)

    def sort_block(b):
        rows = [plan_ref[axis, b : b + 1] for axis in (2, 3, 4)]
        panel = jnp.concatenate([modes_ref[:, b * block : (b + 1) * block].astype(F32), *rows, pad], axis=0)
        row = plan_ref[0, b : b + 1]
        left = jnp.concatenate([jnp.where(row == q, panel, 0.0).astype(BF16) for q in range(sites // 4)], axis=0)
        right = (slot_iota == plan_ref[1, b : b + 1]).astype(F32).astype(BF16)
        return lax.dot_general(left, right, NT, preferred_element_type=F32)

    for pair in range(blocks // 2):
        even, odd = sort_block(2 * pair), sort_block(2 * pair + 1)
        for p in range(sites):
            rows = slice((p // 4) * PANEL, (p // 4) * PANEL + PANEL)
            lanes = slice((p % 4) // 2 * 128, (p % 4) // 2 * 128 + 128)
            low, high = even[rows, lanes], odd[rows, lanes]
            if p % 2:
                low = pltpu.roll(low, CAPACITY, 1)
            else:
                high = pltpu.roll(high, CAPACITY, 1)
            total = jnp.where(low_lanes, low, high)
            start = (p % 2) * STRIDE + 128 * pair
            for part in range(3):
                piece = total[8 * part : 8 * part + 8].astype(BF16)
                out_ref[p // 2, :, start + part * SLOTS : start + part * SLOTS + 128] = piece
            for axis in range(3):
                cell_ref[p, pair : pair + 1, 128 * axis : 128 * axis + 128] = total[24 + axis : 25 + axis]
    for p in range(sites):
        start = (p % 2) * STRIDE + 3 * SLOTS
        out_ref[p // 2, :, start : start + 384] = cell_ref[p].astype(BF16)


def bucket(modes, meta, sites, block):
    plan = pl.pallas_call(
        functools.partial(rank_kernel, sites, block),
        out_shape=jax.ShapeDtypeStruct((5, meta.shape[0], block), F32),
        in_specs=[pl.BlockSpec(memory_space=pltpu.VMEM)],
        out_specs=pl.BlockSpec(memory_space=pltpu.VMEM),
        compiler_params=pltpu.CompilerParams(vmem_limit_bytes=16 * 2**20),
        cost_estimate=pl.CostEstimate(flops=10**9, bytes_accessed=300000, transcendentals=0),
    )(meta)
    return pl.pallas_call(
        bucket_kernel,
        out_shape=jax.ShapeDtypeStruct((sites // 2, 8, 2 * STRIDE), BF16),
        in_specs=[pl.BlockSpec(memory_space=pltpu.VMEM)] * 2,
        out_specs=pl.BlockSpec(memory_space=pltpu.VMEM),
        scratch_shapes=[pltpu.VMEM((sites, 8, 384), F32)],
        compiler_params=pltpu.CompilerParams(vmem_limit_bytes=48 * 2**20),
        cost_estimate=pl.CostEstimate(flops=4 * 10**9, bytes_accessed=1500000, transcendentals=0),
    )(modes, plan)


def table_row(row):
    return row if row < HALF else row + 1


def fill_steps(panel_ref, base, trig_ref, left_ref, right_ref):
    width = SLOTS
    loaded = []

    def lookup():
        lines = panel_ref[:, base + 3 * SLOTS : base + STRIDE].astype(F32)
        cells = [
            jnp.concatenate([lines[row : row + 1, 128 * axis : 128 * axis + 128] for row in range(8)], axis=1)
            for axis in range(3)
        ]
        rows = lax.broadcasted_iota(I32, (24, width), 0).astype(F32)
        starts = ((0, 12, 16), (24, 48, 24), (72, 88, 16))
        for axis, (cos_start, sin_start, count) in enumerate(starts):
            turn = rows[:count] * (cells[axis] * (1.0 / EDGE))
            turn = turn - jnp.round(turn)
            square = turn * turn
            cos, sin = horner(COSINE, square), horner(SINE, square) * turn
            if axis == 0:
                cos, sin = cos[:HALF], sin[:HALF]
            trig_ref[cos_start : cos_start + cos.shape[0]] = cos
            trig_ref[sin_start : sin_start + sin.shape[0]] = sin

    def left(pair):
        if not loaded:
            parts = [panel_ref[:, base + SLOTS * part : base + SLOTS * part + SLOTS] for part in range(3)]
            loaded.append(jnp.concatenate([part.astype(F32) for part in parts], axis=0))
        values = loaded[0]
        row = table_row(ORDER[2 * pair])
        first = values * trig_ref[row : row + 1]
        if pair < HALF - 1:
            row = table_row(ORDER[2 * pair + 1])
            second = values * trig_ref[row : row + 1]
        else:
            second = jnp.zeros((8, width), F32)
        both = jnp.concatenate([first, second], axis=0).astype(BF16)
        left_ref[48 * pair : 48 * pair + both.shape[0]] = both

    def plane(wave, low, high):
        cos1, sin1 = trig_ref[24 + low : 24 + high], trig_ref[48 + low : 48 + high]
        cos2, sin2 = trig_ref[72 + wave : 73 + wave], trig_ref[88 + wave : 89 + wave]
        return cos1 * cos2 - sin1 * sin2, sin1 * cos2 + cos1 * sin2

    def right(pair):
        parts = [plane(wave, 0, 24) for wave in (2 * pair + 1, 2 * pair + 2)]
        for part in range(2):
            both = jnp.concatenate([parts[0][part], parts[1][part]], axis=0).astype(BF16)
            right_ref[MAIN * part + 48 * pair : MAIN * part + 48 * pair + 48] = both

    def right_last():
        parts = plane(HALF - 1, 0, 16)
        for part in range(2):
            right_ref[MAIN * part + 240 : MAIN * part + 256] = parts[part].astype(BF16)

    def side():
        cos, sin = plane(HALF - 1, 16, 24)
        base = jnp.concatenate([trig_ref[24:40], cos, trig_ref[48:64], sin], axis=0)
        for block, row in enumerate(map(table_row, FINE)):
            start = 2 * MAIN + SIDE * block
            right_ref[start : start + SIDE] = (base * trig_ref[row : row + 1]).astype(BF16)

    steps = [lookup] + [functools.partial(left, pair) for pair in range(HALF)]
    return steps + [functools.partial(right, pair) for pair in range(5)] + [right_last, side]


def project_kernel(
    norm, panel_ref, wave_ref, out_ref, trig_ref, left0, left1, right0, right1, acc_ref, side_ref, power_ref
):
    lefts, rights = (left0, left1), (right0, right1)
    sources, places = panel_ref.shape[0], 2
    for right in rights:
        right[2 * MAIN + 5 * SIDE :] = jnp.zeros((256 - 5 * SIDE, right.shape[1]), BF16)
    dests = out_ref.shape[0]
    width = out_ref.shape[3]
    first, second, third = split_flat(wave_ref[...].astype(F32))
    flip0 = first > HALF - 1
    flip12 = (third > HALF - 1) | ((third == 0) & (second > HALF - 1))
    wave0 = jnp.where(flip0, EDGE - first, first)
    wave1 = jnp.where(flip12 & (second > 0), EDGE - second, second)
    wave2 = jnp.where(flip12 & (third > 0), EDGE - third, third)
    group = wave0 * 2.0 + (flip0 != flip12).astype(F32)
    side_row = (group >= SIDE_GROUPS).astype(F32) + (group >= 2 * SIDE_GROUPS).astype(F32)
    in_side = (wave2 == 0) | ((wave2 == HALF - 1) & (wave1 > 15))
    column = jnp.where(in_side, (group - SIDE_GROUPS * side_row) * 24.0, (wave2 - 1.0) * 24.0) + wave1
    group = jnp.where(in_side, 2.0 * HALF + side_row, group)
    row_iota = lax.broadcasted_iota(I32, (MAIN, width), 0).astype(F32)
    lane_iota = lax.broadcasted_iota(I32, (24, 256), 1)
    scale = 1.0 / norm

    def steps_of(chunk):
        slot = chunk % 2
        base = chunk // sources * STRIDE
        return fill_steps(panel_ref.at[chunk % sources], base, trig_ref.at[slot], lefts[slot], rights[slot])

    def powers(cc, cs, sc, ss):
        return ((cc - ss) ** 2 + (cs + sc) ** 2) * scale, ((cc + ss) ** 2 + (cs - sc) ** 2) * scale

    def square(place):
        for wave in range(HALF):
            start = 24 * ORDER.index(wave)
            cc, cs = acc_ref[place, start : start + 24, :MAIN], acc_ref[place, start : start + 24, MAIN:]
            sc = ss = jnp.zeros_like(cc)
            if wave:
                start = 24 * ORDER.index(11 + wave)
                sc, ss = acc_ref[place, start : start + 24, :MAIN], acc_ref[place, start : start + 24, MAIN:]
            power_ref[48 * wave : 48 * wave + 48] = jnp.concatenate(powers(cc, cs, sc, ss), axis=0).astype(BF16)

    def square_side(place):
        blocks = []
        for row in range(5):
            whole = side_ref[place, 24 * row : 24 * row + 24]
            shifted = [whole] + [pltpu.roll(whole, 256 - SIDE * block, 1) for block in range(1, 5)]
            blocks.append([piece[:, :128] for piece in shifted])
        packed = [jnp.zeros((24, 256), F32) for _ in range(3)]
        for wave in range(HALF):
            coarse = (wave + 2) // 5
            fine = wave - 5 * coarse
            far, near, sign = 2 * coarse, 2 * abs(fine), 1.0 if fine > 0 else -1.0
            if not coarse:
                cos = blocks[0][max(near - 1, 0)]
                sin = blocks[0][near] if near else jnp.zeros_like(cos)
            elif not fine:
                cos, sin = blocks[far - 1][0], blocks[far][0]
            else:
                cos = blocks[far - 1][near - 1] - sign * blocks[far][near]
                sin = blocks[far][near - 1] + sign * blocks[far - 1][near]
            both = powers(cos, pltpu.roll(cos, 128 - 24, 1), sin, pltpu.roll(sin, 128 - 24, 1))
            for flipped in range(2):
                index = 2 * wave + flipped
                wide = jnp.concatenate([both[flipped], jnp.zeros((24, 128), F32)], axis=1)
                wide = jnp.where(lane_iota < 24, wide, 0.0)
                at = 24 * (index % SIDE_GROUPS)
                packed[index // SIDE_GROUPS] += pltpu.roll(wide, at, 1) if at else wide
        rows = jnp.concatenate(packed + [jnp.zeros((8, 256), F32)], axis=0)
        power_ref[576:656] = rows.astype(BF16)

    def pick(dest):
        chosen = (row_iota == column[dest : dest + 1]).astype(F32).astype(BF16)
        return jnp.dot(power_ref[...], chosen, preferred_element_type=F32)

    def store(place, dest, picked):
        total = jnp.zeros((24, width), F32)
        for g in range(2 * HALF + 3):
            total += jnp.where(group[dest : dest + 1] == g, picked[24 * g : 24 * g + 24], 0.0)
        out_ref[dest, place] = total.astype(BF16)

    def finish(place):
        square(place)
        square_side(place)
        picked = pick(0)
        for dest in range(dests):
            following = pick(dest + 1) if dest + 1 < dests else None
            store(place, dest, picked)
            picked = following

    chunks = places * sources
    for step in steps_of(0):
        step()
    for chunk in range(chunks):
        slot = chunk % 2
        left, right = lefts[slot], rights[slot]
        product = lax.dot_general(left[...], right[: 2 * MAIN], NT, preferred_element_type=F32)
        side = lax.dot_general(left[:128], right[2 * MAIN :], NT, preferred_element_type=F32)
        for step in steps_of(chunk + 1) if chunk + 1 < chunks else []:
            step()
        place = chunk // sources
        if chunk % sources == 0:
            acc_ref[place] = product
            side_ref[place] = side
        else:
            acc_ref[place] += product
            side_ref[place] += side
        if (chunk + 1) % sources == 0:
            finish(place)


def project(panel, waves, norm):
    places, slots = 2, SLOTS
    return pl.pallas_call(
        functools.partial(project_kernel, norm),
        out_shape=jax.ShapeDtypeStruct((waves.shape[0], places, 24, waves.shape[1]), BF16),
        in_specs=[pl.BlockSpec(memory_space=pltpu.VMEM)] * 2,
        out_specs=pl.BlockSpec(memory_space=pltpu.VMEM),
        scratch_shapes=[
            pltpu.VMEM((2, 104, slots), F32),
            pltpu.VMEM((ROWS_LHS, slots), BF16),
            pltpu.VMEM((ROWS_LHS, slots), BF16),
            pltpu.VMEM((2 * MAIN + 256, slots), BF16),
            pltpu.VMEM((2 * MAIN + 256, slots), BF16),
            pltpu.VMEM((places, ROWS_LHS, 2 * MAIN), F32),
            pltpu.VMEM((places, 128, 256), F32),
            pltpu.VMEM((656, MAIN), BF16),
        ],
        compiler_params=pltpu.CompilerParams(vmem_limit_bytes=48 * 2**20),
        cost_estimate=pl.CostEstimate(flops=18 * 10**9, bytes_accessed=2000000, transcendentals=0),
    )(panel, waves)


def body(modes, atom_site, site_owner, translation, wavevectors):
    col_count = lax.axis_size("col")
    sites = site_owner.shape[0]
    atoms = translation.shape[0]
    norm = 3.0 * atoms * col_count / 2.0
    message = [
        atom_site[:, 0] * 2**CELL_BITS + translation,
        wavevectors,
        jnp.pad(site_owner, (0, 128 - sites)),
    ]
    packed = jnp.concatenate(message)
    packed = jnp.broadcast_to(packed[None], (col_count, packed.shape[0]))
    meta = lax.all_to_all(packed, "col", split_axis=0, concat_axis=0, tiled=True)
    waves = meta[:, atoms : atoms + wavevectors.shape[0]]
    buckets = bucket(modes, meta, sites, atoms)
    panel = lax.all_to_all(buckets, "row", split_axis=0, concat_axis=0, tiled=True)
    power = project(panel, waves, norm)
    arrived = lax.all_to_all(power, "col", split_axis=0, concat_axis=0, tiled=True)
    arrived = arrived.transpose(1, 0, 2, 3).reshape(2, 3, -1, wavevectors.shape[0])
    projected = jnp.sum(arrived.astype(F32), axis=1)
    local = jnp.sum(projected, axis=0).reshape(lax.axis_size("row"), -1, wavevectors.shape[0])
    shares = lax.all_to_all(local, "row", split_axis=0, concat_axis=0, tiled=True)
    return projected, jnp.sum(shares, axis=0) * (1.0 / sites)


def solution(mesh):
    placed = (P("col", "row"), P(("row", "col"), None), P(), P(("row", "col")), P("col"))
    return jax.shard_map(
        body,
        mesh=mesh,
        in_specs=placed,
        out_specs=(P("row", None, "col"), P("row", "col")),
        check_vma=False,
    )
```
